512 devices in a mesh: dp: 8 (over x, core), ctx: 64 (over y, z).
Axes of the slice: x: 4, y: 8, z: 8, core: 2. Of those that a mesh axis runs over, the one named last changes fastest.
Arguments:
- token_ids: int32 [8, 8192], P('dp', 'ctx'), may hold values from 0 to 7
- queries: bfloat16 [8, 8192, 4096], P('dp', 'ctx'), may hold values from -6 to 6
- gated_values: bfloat16 [8, 8192, 4096], P('dp', 'ctx'), may hold values from -6 to 6
- out_grad: bfloat16 [8, 8192, 4096], P('dp', 'ctx'), may hold values from -6 to 6
- filters: bfloat16 [4096, 128], P('ctx'), may hold values from -0.5 to 0.5
Outputs:
- value_grad: bfloat16 [8, 8192, 4096], P('dp', 'ctx')
- filter_grad: float32 [4096, 128], P('ctx')
The draws below stay inside these ranges and needn't reach their ends.
Inputs may be any that keep to these rules, and one draw needn't show every extreme that they name: `token_ids`: ids 0 to 3 are upper-case bases, 4 to 7 lower-case bases.
All inputs are finite; a program needn't handle non-finite values.
Results may differ from the reference program's by a relative error of at most 0.0049.
Values may be sent and summed in bfloat16 or wider, within the bound.
A program may use at most 64 MiB of HBM per device.

```python
import jax
import jax.numpy as jnp
from jax import lax

D = 4096
TAPS = 128
LENGTH = 8192
SEQS = 8
ALLTOK = 65536


def plant(values, stream_key, least, top_value):
    place = [jax.random.randint(jax.random.fold_in(stream_key, axis), (), 0, length) for axis, length in enumerate(values.shape)]
    widest = values.shape.index(max(values.shape))
    beside = place[:widest] + [(place[widest] + 1) % values.shape[widest]] + place[widest + 1:]
    return values.at[tuple(place)].set(least).at[tuple(beside)].set(top_value)


def levels(own_key, extent, pieces, least, high):
    level, own = 1.0, jax.random.fold_in(own_key, 6)
    for axis_at, blocks in pieces:
        steps = jnp.exp(jax.random.uniform(jax.random.fold_in(own, axis_at), (blocks,), jnp.float32, least / len(pieces), high / len(pieces)))
        level = level * jnp.repeat(steps, extent[axis_at] // blocks).reshape([-1 if axis == axis_at else 1 for axis in range(len(extent))])
    return level


def noise(stream_key, dims, width, reach, cuts=(), held_as=jnp.bfloat16):
    values = width * jax.random.normal(stream_key, dims, jnp.float32)
    if cuts:
        values = values * levels(stream_key, dims, cuts, -0.22, 0.18)
    return jnp.clip(values, -reach, reach).astype(held_as)


def setup_inputs(seed: int = 0) -> dict:
    streams_of = jax.random.split(jax.random.key(seed), 6)
    token_ids = plant(jax.random.randint(streams_of[0], (SEQS, LENGTH), 0, 8), jax.random.fold_in(streams_of[0], 1), 0, 7).astype(jnp.int32)
    queries = noise(streams_of[1], (SEQS, LENGTH, D), 1.0, 6.0, ((0, 8), (1, 64)))
    gated_values = noise(streams_of[2], (SEQS, LENGTH, D), 1.0, 6.0, ((0, 8), (1, 64)))
    out_grad = noise(streams_of[3], (SEQS, LENGTH, D), 1.0, 6.0, ((0, 8), (1, 64)))
    filters = noise(streams_of[4], (D, TAPS), TAPS ** -0.5, 0.5, ((0, 64),))
    return dict(token_ids=token_ids, queries=queries, gated_values=gated_values, out_grad=out_grad, filters=filters)


def reference(token_ids, queries, gated_values, out_grad, filters):
    weight = jnp.where(token_ids < 4, 1.0, 0.1).astype(jnp.float32)
    product = weight[:, :, None] * out_grad.astype(jnp.float32) * queries.astype(jnp.float32)
    cotangent = lax.optimization_barrier(product.astype(jnp.bfloat16)).astype(jnp.float32)
    span = 2 * LENGTH
    filter_freq = jnp.fft.rfft(filters.T.astype(jnp.float32), n=span, axis=0)

    def per_sequence(pair):
        cot_seq, val_seq = pair
        cot_freq = jnp.fft.rfft(cot_seq, n=span, axis=0)
        val_freq = jnp.fft.rfft(val_seq.astype(jnp.float32), n=span, axis=0)
        grad_seq = jnp.fft.irfft(cot_freq * jnp.conj(filter_freq), n=span, axis=0)[:LENGTH]
        tap_seq = jnp.fft.irfft(cot_freq * jnp.conj(val_freq), n=span, axis=0)[:TAPS]
        return grad_seq.astype(jnp.float32).astype(jnp.bfloat16), tap_seq.astype(jnp.float32)

    value_grad, tap_terms = lax.map(per_sequence, (cotangent, gated_values))
    filter_grad = (jnp.sum(tap_terms, axis=0).T * (ALLTOK ** -0.5)).astype(jnp.float32)
    return value_grad, filter_grad
```

```python
import jax
import jax.numpy as jnp
import numpy as np
from jax import lax
from jax.sharding import PartitionSpec as P


def tables(span):
    half = span // 2
    angle = np.pi * (2 * np.arange(half)[:, None] + 1) * np.arange(span)[None, :] / span
    wave = np.concatenate([np.cos(angle), np.sin(angle)], axis=0)
    high = wave.astype(jnp.bfloat16)
    low = (wave - high.astype(np.float64)).astype(jnp.bfloat16)
    return high, low


def mul(a, b):
    return jnp.dot(a, b, preferred_element_type=jnp.float32)


def body(token_ids, queries, gated_values, out_grad, filters):
    dp, ctx = lax.axis_size("dp"), lax.axis_size("ctx")
    weight = jnp.where(token_ids < 4, 1.0, 0.1).astype(jnp.float32)
    cotangent = (
        weight[:, :, None] * out_grad.astype(jnp.float32) * queries.astype(jnp.float32)
    ).astype(jnp.bfloat16)[0]
    rows = cotangent.shape[0]
    factor_tok = float(dp * ctx * rows) ** (-0.5)
    taps = lax.all_gather(filters, "ctx", axis=0, tiled=True)
    after = lax.ppermute(cotangent, "ctx", [(i, i - 1) for i in range(1, ctx)])
    high, low = (jnp.asarray(t) for t in tables(2 * rows))

    def forward(x):
        n = x.shape[0]
        wave = mul(high[:, :n], x) + mul(low[:, :n], x)
        return wave[:rows], wave[rows:]

    def backward(re, im):
        both = jnp.concatenate([re, im], axis=0) * (1.0 / rows)
        top = both.astype(jnp.bfloat16)
        rest = (both - top.astype(jnp.float32)).astype(jnp.bfloat16)
        up, down = high[:, :rows].T, low[:, :rows].T
        return mul(up, top) + (mul(up, rest) + mul(down, top))

    cot_cos, cot_sin = forward(jnp.concatenate([cotangent, after], axis=0))

    def correlate(x):
        x_cos, x_sin = forward(x)
        return backward(cot_cos * x_cos + cot_sin * x_sin, cot_sin * x_cos - cot_cos * x_sin)

    tap_part = correlate(gated_values[0]).T * factor_tok
    filter_grad = lax.psum(lax.psum_scatter(tap_part, "ctx", scatter_dimension=0, tiled=True), "dp")
    value_grad = correlate(taps.T).astype(jnp.bfloat16)[None]
    return value_grad, filter_grad


def solution(mesh):
    return jax.shard_map(
        body,
        mesh=mesh,
        in_specs=(
            P("dp", "ctx"),
            P("dp", "ctx", None),
            P("dp", "ctx", None),
            P("dp", "ctx", None),
            P("ctx", None),
        ),
        out_specs=(P("dp", "ctx", None), P("ctx", None)),
        check_vma=False,
    )
```

```python
import functools

import jax
import jax.numpy as jnp
import numpy as np
from jax import lax
from jax.experimental import pallas as pl
from jax.experimental.pallas import tpu as pltpu
from jax.sharding import PartitionSpec as P

F32, BF16 = jnp.float32, jnp.bfloat16
SIDES = {64: (8, 8)}


def tables(rows):
    span = 2 * rows
    angle = np.pi * (2 * np.arange(rows)[:, None] + 1) * np.arange(span)[None, :] / span
    wave = np.concatenate([np.cos(angle), np.sin(angle)], axis=0)
    high = wave.astype(BF16)
    low = (wave - high.astype(np.float64)).astype(BF16)
    own = np.concatenate([high[:, :rows], low[:, :rows]], axis=1)
    after = np.concatenate([high[:, rows:], low[:, rows:]], axis=1)
    back = np.concatenate([high[:, :rows].T, low[:, :rows].T], axis=0)
    back = (back.astype(np.float64) / rows).astype(BF16)
    return np.concatenate([own, after, back], axis=0)


def mul(a, b):
    return jnp.dot(a, b, preferred_element_type=F32)


def twice(x):
    return jnp.concatenate([x, x], axis=0)


def kernel(
    nx, ny, nz, scale,
    tok, q_hbm, gv_hbm, og_hbm, filt_hbm, tab_hbm,
    v_hbm, g_hbm,
    q_v, og_v, gv_v, tab, w_v, cot, halo, cspec, gspec, fbuf, v_v,
    gst, r0, s0, r1, s1, r2, s2, r3, fg,
    lsem, osem, ssem, rsem,
):
    rows = q_v.shape[0]
    chunks = nz // 2
    pairs = ny // 2
    dp, ctx = lax.axis_index("dp"), lax.axis_index("ctx")
    x, c = dp // 2, dp % 2
    y, z = ctx // nz, ctx % nz
    nctx, ndp = ny * nz, 2 * nx
    part = 64 // ndp
    frows = pl.ds(pl.multiple_of(x * (64 // nx), 16), 64 // nx)

    barrier = pltpu.get_barrier_semaphore()
    peers = [{"ctx": (ctx + 1) % nctx}, {"ctx": (ctx + nctx - 1) % nctx}]
    peers += [{"dp": (dp + d) % ndp} for d in range(1, ndp)]
    peers += [{"ctx": ((y + d) % ny) * nz + z} for d in range(1, ny)]
    peers += [{"ctx": y * nz + (z + d) % nz} for d in range(1, nz)]
    for peer in peers:
        pl.semaphore_signal(barrier, inc=1, device_id=peer, device_id_type=pl.DeviceIdType.MESH)

    loads = [
        pltpu.make_async_copy(q_hbm, q_v, lsem.at[0]),
        pltpu.make_async_copy(og_hbm, og_v, lsem.at[1]),
        pltpu.make_async_copy(filt_hbm.at[frows], fbuf.at[y, z, frows], lsem.at[2]),
        pltpu.make_async_copy(tab_hbm, tab, lsem.at[3]),
        pltpu.make_async_copy(gv_hbm, gv_v, lsem.at[4]),
    ]
    for load in loads:
        load.start()

    started = []

    def send(src, dst, **where):
        n = len(started)
        copy = pltpu.make_async_remote_copy(
            src_ref=src, dst_ref=dst, send_sem=ssem.at[n], recv_sem=rsem.at[n],
            device_id=where, device_id_type=pl.DeviceIdType.MESH,
        )
        copy.start()
        started.append(copy)
        return copy

    def arrive(copies):
        for copy in copies:
            copy.wait_recv()

    def cols(p, i):
        return pl.ds(pl.multiple_of(i * (nz * 64) + p * 128, 128), 128)

    weight = jnp.where(tok[...] < 4, 1.0, 0.1).astype(F32)
    w_v[...] = jnp.broadcast_to(weight, (rows, rows)).T

    def make_cot(p):
        @pl.loop(0, ny)
        def _(i):
            at = cols(p, i)
            cot[p, i] = (w_v[...] * og_v[:, at].astype(F32) * q_v[:, at].astype(F32)).astype(BF16)

    def send_halo(p):
        return send(cot.at[p], halo.at[p], ctx=(ctx + nctx - 1) % nctx)

    own, after = pl.ds(0, 2 * rows), pl.ds(2 * rows, 2 * rows)
    back, back_high = pl.ds(4 * rows, 2 * rows), pl.ds(4 * rows, rows)

    def correlate(wave, other):
        a, b = wave[:rows], wave[rows:]
        e, f = other[:rows], other[rows:]
        both = jnp.concatenate([a * e + b * f, b * e - a * f], axis=0)
        top = both.astype(BF16)
        rest = (both - top.astype(F32)).astype(BF16)
        full = mul(tab[back, :], top)
        return full[:rows] + full[rows:] + mul(tab[back_high, :], rest)

    def spectra(p):
        @pl.loop(0, pairs)
        def _(k):
            cspec[p, k] = mul(tab[own, :], twice(jnp.concatenate([cot[p, 2 * k], cot[p, 2 * k + 1]], axis=1)))
            gv = jnp.concatenate([gv_v[:, cols(p, 2 * k)], gv_v[:, cols(p, 2 * k + 1)]], axis=1)
            gspec[p, k] = mul(tab[own, :], twice(gv))

    live = jnp.where(ctx == nctx - 1, 0.0, 1.0).astype(F32)

    def tap_sums(p):
        @pl.loop(0, pairs)
        def _(k):
            far = mul(tab[after, :], twice(jnp.concatenate([halo[p, 2 * k], halo[p, 2 * k + 1]], axis=1)))
            wave = cspec[p, k] + live * far
            cspec[p, k] = wave
            taps = correlate(wave, gspec[p, k])
            for h in range(2):
                turned = taps[:, 128 * h:128 * (h + 1)].T
                for zz in range(2):
                    for xi in range(nx):
                        for ci in range(2):
                            at = zz * 64 + (2 * xi + ci) * part
                            gst[p, ci, xi, 2 * k + h, zz] = turned[at:at + part]

    def values(p):
        @pl.loop(0, pairs)
        def _(k):
            f = jnp.concatenate(
                [fbuf[2 * k + h, 2 * p + zz] for h in range(2) for zz in range(2)], axis=0
            )
            fwave = lax.dot_general(
                tab[own, :], jnp.concatenate([f, f], axis=1), (((1,), (1,)), ((), ())),
                preferred_element_type=F32,
            )
            out = correlate(cspec[p, k], fwave).astype(BF16)
            for h in range(2):
                v_v[:, cols(p, 2 * k + h)] = out[:, 128 * h:128 * (h + 1)]

        stores = []
        for i in range(ny):
            at = cols(p, i)
            stores.append(pltpu.make_async_copy(v_v.at[:, at], v_hbm.at[:, at], osem.at[p, i]))
            stores[-1].start()
        return stores

    def pair_stage(p):
        return [send(gst.at[p, 1 - c], r0.at[p], dp=2 * x + 1 - c)]

    def x_stage(p):
        for xi in range(nx):
            s0[p, xi] = gst[p, c, xi] + r0[p, xi]
        return [
            send(s0.at[p, (x + d) % nx], r1.at[p, d - 1], dp=2 * ((x + d) % nx) + c)
            for d in range(1, nx)
        ]

    def y_stage(p):
        total = s0[p, x]
        for d in range(1, nx):
            total = total + r1[p, d - 1]
        s1[p] = total
        return [
            send(s1.at[p, (y + d) % ny], r2.at[p, d - 1], ctx=((y + d) % ny) * nz + z)
            for d in range(1, ny)
        ]

    def y_total(p):
        total = s1[p, y]
        for d in range(1, ny):
            total = total + r2[p, d - 1]
        s2[p] = total

    loads[0].wait()
    loads[1].wait()
    make_cot(0)
    loads[2].wait()
    pl.semaphore_wait(barrier, len(peers))

    halos = [send_halo(0)]
    fz = [
        send(fbuf.at[y, z, frows], fbuf.at[y, z, frows], ctx=y * nz + (z + d) % nz)
        for d in range(1, nz)
    ]
    for p in range(1, chunks):
        make_cot(p)
        halos.append(send_halo(p))
    loads[3].wait()
    loads[4].wait()
    spectra(0)
    arrive(fz)
    fy = [
        send(fbuf.at[y, :, frows], fbuf.at[y, :, frows], ctx=((y + d) % ny) * nz + z)
        for d in range(1, ny)
    ]
    for p in range(1, chunks):
        spectra(p)

    xs, ys, stores = {}, {}, []
    for p in range(chunks):
        arrive([halos[p]])
        tap_sums(p)
        first = pair_stage(p)
        if p == 0:
            arrive(fy)
            fx = [
                send(fbuf.at[:, :, frows], fbuf.at[:, :, frows], dp=2 * ((x + d) % nx) + c)
                for d in range(1, nx)
            ]
        else:
            arrive(xs[p - 1])
            ys[p - 1] = y_stage(p - 1)
        arrive(first)
        xs[p] = x_stage(p)
        if p == chunks - 2:
            arrive(fx)
            stores += values(0)
    last = chunks - 1
    if chunks == 1:
        arrive(fx)
        stores += values(0)
    if chunks > 1:
        stores += values(1)
    arrive(xs[last])
    ys[last] = y_stage(last)
    for p in range(2, chunks - 1):
        stores += values(p)
    for p in range(chunks):
        arrive(ys[p])
        y_total(p)
    zs = []
    for d in range(1, nz):
        zi = (z + d) % nz
        zs.append(send(s2.at[zi // 2, zi % 2], r3.at[d - 1], ctx=y * nz + zi))
    if chunks > 2:
        stores += values(last)
    arrive(zs)
    total = s2[z // 2, z % 2]
    for d in range(1, nz):
        total = total + r3[d - 1]
    fg[dp] = total * scale
    ds = [send(fg.at[dp], fg.at[dp], dp=(dp + d) % ndp) for d in range(1, ndp)]
    arrive(ds)
    result = pltpu.make_async_copy(fg, g_hbm, lsem.at[5])
    result.start()
    for copy in started:
        copy.wait_send()
    for store in stores:
        store.wait()
    result.wait()


def body(token_ids, queries, gated_values, out_grad, filters):
    ndp, nctx = lax.axis_size("dp"), lax.axis_size("ctx")
    ny, nz = SIDES[nctx]
    nx = ndp // 2
    _, rows, wide = queries.shape
    assert wide == 64 * nctx and rows == 128
    chunks, pairs, part = nz // 2, ny // 2, 64 // ndp
    scale = float(ndp * nctx * rows) ** (-0.5)
    any_space = pl.BlockSpec(memory_space=pl.ANY)
    remote = (nz // 2) * (1 + 1 + (nx - 1) + (ny - 1)) + 2 * (nz - 1) + (ny - 1) + (nx - 1) + (ndp - 1)
    value_grad, filter_grad = pl.pallas_call(
        functools.partial(kernel, nx, ny, nz, scale),
        out_shape=(
            jax.ShapeDtypeStruct((rows, wide), BF16),
            jax.ShapeDtypeStruct((ndp, part, rows), F32),
        ),
        in_specs=[pl.BlockSpec(memory_space=pltpu.VMEM)] + [any_space] * 5,
        out_specs=(any_space, any_space),
        scratch_shapes=[
            pltpu.VMEM((rows, wide), BF16),
            pltpu.VMEM((rows, wide), BF16),
            pltpu.VMEM((rows, wide), BF16),
            pltpu.VMEM((6 * rows, 2 * rows), BF16),
            pltpu.VMEM((rows, rows), F32),
            pltpu.VMEM((chunks, ny, rows, 128), BF16),
            pltpu.VMEM((chunks, ny, rows, 128), BF16),
            pltpu.VMEM((chunks, pairs, 2 * rows, 256), F32),
            pltpu.VMEM((chunks, pairs, 2 * rows, 256), F32),
            pltpu.VMEM((ny, nz, 64, rows), BF16),
            pltpu.VMEM((rows, wide), BF16),
            pltpu.VMEM((chunks, 2, nx, ny, 2, part, rows), F32),
            pltpu.VMEM((chunks, nx, ny, 2, part, rows), F32),
            pltpu.VMEM((chunks, nx, ny, 2, part, rows), F32),
            pltpu.VMEM((chunks, max(nx - 1, 1), ny, 2, part, rows), F32),
            pltpu.VMEM((chunks, ny, 2, part, rows), F32),
            pltpu.VMEM((chunks, ny - 1, 2, part, rows), F32),
            pltpu.VMEM((chunks, 2, part, rows), F32),
            pltpu.VMEM((nz - 1, part, rows), F32),
            pltpu.VMEM((ndp, part, rows), F32),
            pltpu.SemaphoreType.DMA((6,)),
            pltpu.SemaphoreType.DMA((chunks, ny)),
            pltpu.SemaphoreType.DMA((remote,)),
            pltpu.SemaphoreType.DMA((remote,)),
        ],
        compiler_params=pltpu.CompilerParams(
            collective_id=0, has_side_effects=True, vmem_limit_bytes=48 * 1024 * 1024
        ),
        name="mixer_backward",
    )(
        token_ids, queries[0], gated_values[0], out_grad[0], filters, jnp.asarray(tables(rows)),
    )
    return value_grad[None], filter_grad.reshape(64, rows)


def solution(mesh):
    return jax.shard_map(
        body,
        mesh=mesh,
        in_specs=(
            P("dp", "ctx"),
            P("dp", "ctx", None),
            P("dp", "ctx", None),
            P("dp", "ctx", None),
            P("ctx", None),
        ),
        out_specs=(P("dp", "ctx", None), P("ctx", None)),
        check_vma=False,
    )
```

```python
import functools

import jax
import jax.numpy as jnp
import numpy as np
from jax import lax
from jax.experimental import pallas as pl
from jax.experimental.pallas import tpu as pltpu
from jax.sharding import PartitionSpec as P

F32, BF16 = jnp.float32, jnp.bfloat16
SIDES = {64: (8, 8)}


def tables(rows):
    span = 2 * rows
    angle = np.pi * (2 * np.arange(rows)[:, None] + 1) * np.arange(span)[None, :] / span
    wave = np.concatenate([np.cos(angle), np.sin(angle)], axis=0)
    high = wave.astype(BF16)
    low = (wave - high.astype(np.float64)).astype(BF16)
    own = np.concatenate([high[:, :rows], low[:, :rows]], axis=1)
    after = np.concatenate([high[:, rows:], low[:, rows:]], axis=1)
    back = np.concatenate([high[:, :rows].T, low[:, :rows].T], axis=0)
    back = (back.astype(np.float64) / rows).astype(BF16)
    return np.concatenate([own, after, back], axis=0)


def mul(a, b):
    return jnp.dot(a, b, preferred_element_type=F32)


def twice(x):
    return jnp.concatenate([x, x], axis=0)


def kernel(
    nx, ny, nz, scale,
    tok, q_hbm, gv_hbm, og_hbm, filt_hbm, tab_hbm,
    v_hbm, g_hbm,
    q_v, og_v, gv_v, tab, w_v, cot, halo, gv_own, gv_in, cspec, gspec, fin, fbuf, v_v,
    gst, r0, s0, r2, s2, r3, fg, g_v,
    lsem, osem, ssem, rsem,
):
    rows = q_v.shape[0]
    chunks = nz // 2
    pairs = ny // 2
    dp, ctx = lax.axis_index("dp"), lax.axis_index("ctx")
    x, c = dp // 2, dp % 2
    y, z = ctx // nz, ctx % nz
    nctx, ndp = ny * nz, 2 * nx
    frows = pl.ds(pl.multiple_of(x * (64 // nx), 16), 64 // nx)
    fhalf = pl.ds(c * (nz // 2), nz // 2)
    down = chunks - chunks // 2
    order = [p for k in range(down) for p in (k, down + k) if p < chunks]

    barrier = pltpu.get_barrier_semaphore()
    peers = [{"ctx": (ctx + 1) % nctx}, {"ctx": (ctx + nctx - 1) % nctx}]
    peers += [{"dp": (dp + d) % ndp} for d in range(1, ndp)]
    peers += [{"ctx": ((y + d) % ny) * nz + z} for d in range(1, ny)]
    peers += [{"ctx": y * nz + (z + d) % nz} for d in range(1, nz)]
    for peer in peers:
        pl.semaphore_signal(barrier, inc=1, device_id=peer, device_id_type=pl.DeviceIdType.MESH)

    loads = [
        pltpu.make_async_copy(q_hbm, q_v, lsem.at[0]),
        pltpu.make_async_copy(og_hbm, og_v, lsem.at[1]),
        pltpu.make_async_copy(filt_hbm.at[frows], fin.at[z], lsem.at[2]),
        pltpu.make_async_copy(tab_hbm, tab, lsem.at[3]),
        pltpu.make_async_copy(gv_hbm, gv_v, lsem.at[4]),
    ]
    for load in loads:
        load.start()

    started = []

    def send(src, dst, **where):
        n = len(started)
        copy = pltpu.make_async_remote_copy(
            src_ref=src, dst_ref=dst, send_sem=ssem.at[n], recv_sem=rsem.at[n],
            device_id=where, device_id_type=pl.DeviceIdType.MESH,
        )
        copy.start()
        started.append(copy)
        return copy

    def arrive(copies):
        for copy in copies:
            copy.wait_recv()

    def cols(p, i):
        return pl.ds(pl.multiple_of(i * (nz * 64) + p * 128, 128), 128)

    weight = jnp.where(tok[...] < 4, 1.0, 0.1).astype(F32)
    w_v[...] = jnp.broadcast_to(weight, (rows, rows)).T

    def make_cot(p):
        @pl.loop(0, ny)
        def _(i):
            at = cols(p, i)
            cot[p, i] = (w_v[...] * og_v[:, at].astype(F32) * q_v[:, at].astype(F32)).astype(BF16)

    def hold_gv(p):
        @pl.loop(0, ny)
        def _(i):
            gv_own[p - down, i] = gv_v[:, cols(p, i)]

    def halves(src, dst, to):
        return [(src.at[pl.ds(a * pairs, pairs)], dst.at[pl.ds(a * pairs, pairs)], to) for a in range(2)]

    to_before, to_next = (ctx + nctx - 1) % nctx, (ctx + 1) % nctx

    def halo_halves(p):
        return halves(cot.at[p], halo.at[p], to_before)

    def gv_halves(p):
        return halves(gv_own.at[p - down], gv_in.at[p - down], to_next)

    own, after = pl.ds(0, 2 * rows), pl.ds(2 * rows, 2 * rows)
    back, back_high = pl.ds(4 * rows, 2 * rows), pl.ds(4 * rows, rows)

    def product(wave, other):
        a, b = wave[:rows], wave[rows:]
        e, f = other[:rows], other[rows:]
        return jnp.concatenate([a * e + b * f, b * e - a * f], axis=0)

    def inverse(both):
        top = both.astype(BF16)
        rest = (both - top.astype(F32)).astype(BF16)
        full = mul(tab[back, :], top)
        return full[:rows] + full[rows:] + mul(tab[back_high, :], rest)

    def spectra(p):
        @pl.loop(0, pairs)
        def _(k):
            cspec[p, k] = mul(tab[own, :], twice(jnp.concatenate([cot[p, 2 * k], cot[p, 2 * k + 1]], axis=1)))
            gv = jnp.concatenate([gv_v[:, cols(p, 2 * k)], gv_v[:, cols(p, 2 * k + 1)]], axis=1)
            gspec[p, k] = mul(tab[own, :], twice(gv))

    has_next = jnp.where(ctx == nctx - 1, 0.0, 1.0).astype(F32)
    has_before = jnp.where(ctx == 0, 0.0, 1.0).astype(F32)

    def with_halo(p, k):
        far = mul(tab[after, :], twice(jnp.concatenate([halo[p, 2 * k], halo[p, 2 * k + 1]], axis=1)))
        return cspec[p, k] + has_next * far

    def tap_sums(p):
        @pl.loop(0, pairs)
        def _(k):
            if p < down:
                wave = with_halo(p, k)
                cspec[p, k] = wave
                taps = inverse(product(wave, gspec[p, k]))
            else:
                u = p - down
                far = has_before * mul(tab[after, :], twice(jnp.concatenate([cot[p, 2 * k], cot[p, 2 * k + 1]], axis=1)))
                gv = mul(tab[own, :], twice(jnp.concatenate([gv_in[u, 2 * k], gv_in[u, 2 * k + 1]], axis=1)))
                taps = inverse(product(cspec[p, k], gspec[p, k]) + product(far, gv))
            for h in range(2):
                turned = taps[:, 128 * h:128 * (h + 1)].T
                for zz in range(2):
                    for ci in range(2):
                        at = zz * 64 + ci * 32
                        gst[p, ci, 2 * k + h, zz] = turned[at:at + 32]

    def values(p):
        @pl.loop(0, pairs)
        def _(k):
            f = jnp.concatenate(
                [fbuf[2 * k + h, 2 * p + zz] for h in range(2) for zz in range(2)], axis=0
            )
            fwave = lax.dot_general(
                tab[own, :], jnp.concatenate([f, f], axis=1), (((1,), (1,)), ((), ())),
                preferred_element_type=F32,
            )
            wave = cspec[p, k] if p < down else with_halo(p, k)
            out = inverse(product(wave, fwave)).astype(BF16)
            for h in range(2):
                v_v[:, cols(p, 2 * k + h)] = out[:, 128 * h:128 * (h + 1)]

        stores = []
        for i in range(ny):
            at = cols(p, i)
            stores.append(pltpu.make_async_copy(v_v.at[:, at], v_hbm.at[:, at], osem.at[p, i]))
            stores[-1].start()
        return stores

    def pair_stage(p):
        return [send(gst.at[p, 1 - c], r0.at[p], dp=2 * x + 1 - c)]

    def y_stage(p):
        @pl.loop(0, ny)
        def _(i):
            s0[p, i] = (gst[p, c, i] + r0[p, i]).astype(BF16)

        return [
            send(s0.at[p, (y + d) % ny], r2.at[p, d - 1], ctx=((y + d) % ny) * nz + z)
            for d in range(1, ny)
        ]

    def y_total(p):
        total = gst[p, c, y] + r0[p, y]
        for d in range(1, ny):
            total = total + r2[p, d - 1].astype(F32)
        s2[p] = total

    loads[0].wait()
    loads[1].wait()
    for p in range(chunks):
        make_cot(p)
    loads[4].wait()
    for p in range(down, chunks):
        hold_gv(p)
    loads[2].wait()
    loads[3].wait()
    pl.semaphore_wait(barrier, len(peers))

    fz = [send(fin.at[z], fin.at[z], ctx=y * nz + (z + d) % nz) for d in range(1, nz)]
    down_list = [(p, h) for p in range(chunks) for h in halo_halves(p)]
    up_list = [(p, h) for p in range(down, chunks) for h in gv_halves(p)]
    halos, gvs = {p: [] for p in range(chunks)}, {p: [] for p in range(chunks)}

    def issue(todo, done, n):
        for p, (src, dst, to) in todo[:n]:
            done[p].append(send(src, dst, ctx=to))
        del todo[:n]

    for p in order:
        issue(down_list, halos, 1)
        issue(up_list, gvs, 1)
        spectra(p)

    first, ys, stores = {}, {}, []
    for n, p in enumerate(order):
        arrive(halos[p] if p < down else gvs[p])
        issue(down_list, halos, 1)
        issue(up_list, gvs, 1)
        tap_sums(p)
        first[p] = pair_stage(p)
        if n == 0:
            arrive(fz)
            fy = [
                send(fin.at[fhalf], fbuf.at[y, fhalf, frows], ctx=((y + d) % ny) * nz + z)
                for d in range(1, ny)
            ]
            fbuf[y, fhalf, frows] = fin[fhalf]
        if n >= 1:
            arrive(first[order[n - 1]])
            ys[order[n - 1]] = y_stage(order[n - 1])
        if n == min(1, chunks - 1):
            arrive(fy)
            fx = [
                send(fbuf.at[:, fhalf, frows], fbuf.at[:, fhalf, frows], dp=2 * ((x + d) % nx) + c)
                for d in range(1, nx)
            ]
    arrive(first[order[-1]])
    ys[order[-1]] = y_stage(order[-1])
    issue(down_list, halos, len(down_list))
    arrive(fx)
    fc = [send(fbuf.at[:, fhalf], fbuf.at[:, fhalf], dp=2 * x + 1 - c)]
    for p in range(chunks):
        arrive(ys[p])
        y_total(p)
    zs = []
    for d in range(1, nz):
        zi = (z + d) % nz
        zs.append(send(s2.at[zi // 2, zi % 2], r3.at[d - 1], ctx=y * nz + zi))
    arrive(fc)
    for p in range(down):
        stores += values(p)
    arrive(zs)
    total = s2[z // 2, z % 2]
    for d in range(1, nz):
        total = total + r3[d - 1]
    fg[dp] = total * scale
    ds = [send(fg.at[dp], fg.at[dp], dp=(dp + d) % ndp) for d in range(1, ndp)]
    for p in range(down, chunks):
        arrive(halos[p])
        stores += values(p)
    arrive(ds)
    for ci in range(2):
        total = fg[ci]
        for xi in range(1, nx):
            total = total + fg[2 * xi + ci]
        g_v[ci] = total
    result = pltpu.make_async_copy(g_v, g_hbm, lsem.at[5])
    result.start()
    for copy in started:
        copy.wait_send()
    for store in stores:
        store.wait()
    result.wait()


def body(token_ids, queries, gated_values, out_grad, filters):
    ndp, nctx = lax.axis_size("dp"), lax.axis_size("ctx")
    ny, nz = SIDES[nctx]
    nx = ndp // 2
    _, rows, wide = queries.shape
    assert wide == 64 * nctx and rows == 128
    chunks, pairs = nz // 2, ny // 2
    scale = float(ndp * nctx * rows) ** (-0.5)
    any_space = pl.BlockSpec(memory_space=pl.ANY)
    up = chunks // 2
    remote = chunks * (2 + ny) + 2 * up + 2 * (nz - 1) + (ny - 1) + nx + (ndp - 1)
    value_grad, filter_grad = pl.pallas_call(
        functools.partial(kernel, nx, ny, nz, scale),
        out_shape=(
            jax.ShapeDtypeStruct((rows, wide), BF16),
            jax.ShapeDtypeStruct((2, 32, rows), F32),
        ),
        in_specs=[pl.BlockSpec(memory_space=pltpu.VMEM)] + [any_space] * 5,
        out_specs=(any_space, any_space),
        scratch_shapes=[
            pltpu.VMEM((rows, wide), BF16),
            pltpu.VMEM((rows, wide), BF16),
            pltpu.VMEM((rows, wide), BF16),
            pltpu.VMEM((6 * rows, 2 * rows), BF16),
            pltpu.VMEM((rows, rows), F32),
            pltpu.VMEM((chunks, ny, rows, 128), BF16),
            pltpu.VMEM((chunks, ny, rows, 128), BF16),
            pltpu.VMEM((max(up, 1), ny, rows, 128), BF16),
            pltpu.VMEM((max(up, 1), ny, rows, 128), BF16),
            pltpu.VMEM((chunks, pairs, 2 * rows, 256), F32),
            pltpu.VMEM((chunks, pairs, 2 * rows, 256), F32),
            pltpu.VMEM((nz, 64 // nx, rows), BF16),
            pltpu.VMEM((ny, nz, 64, rows), BF16),
            pltpu.VMEM((rows, wide), BF16),
            pltpu.VMEM((chunks, 2, ny, 2, 32, rows), F32),
            pltpu.VMEM((chunks, ny, 2, 32, rows), F32),
            pltpu.VMEM((chunks, ny, 2, 32, rows), BF16),
            pltpu.VMEM((chunks, ny - 1, 2, 32, rows), BF16),
            pltpu.VMEM((chunks, 2, 32, rows), F32),
            pltpu.VMEM((nz - 1, 32, rows), F32),
            pltpu.VMEM((ndp, 32, rows), F32),
            pltpu.VMEM((2, 32, rows), F32),
            pltpu.SemaphoreType.DMA((6,)),
            pltpu.SemaphoreType.DMA((chunks, ny)),
            pltpu.SemaphoreType.DMA((remote,)),
            pltpu.SemaphoreType.DMA((remote,)),
        ],
        compiler_params=pltpu.CompilerParams(
            collective_id=0, has_side_effects=True, vmem_limit_bytes=60 * 1024 * 1024
        ),
        name="mixer_backward",
    )(
        token_ids, queries[0], gated_values[0], out_grad[0], filters, jnp.asarray(tables(rows)),
    )
    return value_grad[None], filter_grad.reshape(64, rows)


def solution(mesh):
    return jax.shard_map(
        body,
        mesh=mesh,
        in_specs=(
            P("dp", "ctx"),
            P("dp", "ctx", None),
            P("dp", "ctx", None),
            P("dp", "ctx", None),
            P("ctx", None),
        ),
        out_specs=(P("dp", "ctx", None), P("ctx", None)),
        check_vma=False,
    )
```

```python
import functools

import jax
import jax.numpy as jnp
import numpy as np
from jax import lax
from jax.experimental import pallas as pl
from jax.experimental.pallas import tpu as pltpu
from jax.sharding import PartitionSpec as P

F32, BF16 = jnp.float32, jnp.bfloat16
SIDES = {64: (8, 8)}


def tables(rows):
    span = 2 * rows
    angle = np.pi * (2 * np.arange(rows)[:, None] + 1) * np.arange(span)[None, :] / span
    wave = np.concatenate([np.cos(angle), np.sin(angle)], axis=0)
    high = wave.astype(BF16)
    low = (wave - high.astype(np.float64)).astype(BF16)
    own = np.concatenate([high[:, :rows], low[:, :rows]], axis=1)
    after = np.concatenate([high[:, rows:], low[:, rows:]], axis=1)
    back = np.concatenate([high[:, :rows].T, low[:, :rows].T], axis=0)
    back = (back.astype(np.float64) / rows).astype(BF16)
    return np.concatenate([own, after, back], axis=0)


def mul(a, b):
    return jnp.dot(a, b, preferred_element_type=F32)


def twice(x):
    return jnp.concatenate([x, x], axis=0)


def kernel(
    nx, ny, nz, scale,
    tok_hbm, q_hbm, gv_hbm, og_hbm, filt_hbm, tab_hbm,
    v_hbm, g_hbm,
    tok, q_v, og_v, gv_v, tab, w_v, cot, halo, gv_own, gv_in, cspec, gspec, fin, fbuf, v_v,
    gst, r0, s0, r2, s2, r3, fg, g_v,
    lsem, osem, ssem, rsem,
):
    rows = q_v.shape[0]
    chunks = nz // 2
    pairs = ny // 2
    dp, ctx = lax.axis_index("dp"), lax.axis_index("ctx")
    x, c = dp // 2, dp % 2
    y, z = ctx // nz, ctx % nz
    nctx, ndp = ny * nz, 2 * nx
    frows = pl.ds(pl.multiple_of(x * (64 // nx), 16), 64 // nx)
    fhalf = pl.ds(c * (nz // 2), nz // 2)
    down = chunks - chunks // 2
    order = [p for k in range(down) for p in (k, down + k) if p < chunks]

    barrier = pltpu.get_barrier_semaphore()
    peers = [{"ctx": (ctx + 1) % nctx}, {"ctx": (ctx + nctx - 1) % nctx}]
    peers += [{"dp": (dp + d) % ndp} for d in range(1, ndp)]
    peers += [{"ctx": ((y + d) % ny) * nz + z} for d in range(1, ny)]
    peers += [{"ctx": y * nz + (z + d) % nz} for d in range(1, nz)]
    for peer in peers:
        pl.semaphore_signal(barrier, inc=1, device_id=peer, device_id_type=pl.DeviceIdType.MESH)

    loads = [
        pltpu.make_async_copy(q_hbm, q_v, lsem.at[0]),
        pltpu.make_async_copy(og_hbm, og_v, lsem.at[1]),
        pltpu.make_async_copy(filt_hbm.at[frows], fin.at[z], lsem.at[2]),
        pltpu.make_async_copy(tab_hbm, tab, lsem.at[3]),
        pltpu.make_async_copy(gv_hbm, gv_v, lsem.at[4]),
        pltpu.make_async_copy(tok_hbm, tok, lsem.at[5]),
    ]
    for load in loads:
        load.start()

    started = []

    def send(src, dst, **where):
        n = len(started)
        copy = pltpu.make_async_remote_copy(
            src_ref=src, dst_ref=dst, send_sem=ssem.at[n], recv_sem=rsem.at[n],
            device_id=where, device_id_type=pl.DeviceIdType.MESH,
        )
        copy.start()
        started.append(copy)
        return copy

    def arrive(copies):
        for copy in copies:
            copy.wait_recv()

    def cols(p, i):
        return pl.ds(pl.multiple_of(i * (nz * 64) + p * 128, 128), 128)

    def make_cot(p):
        @pl.loop(0, ny)
        def _(i):
            at = cols(p, i)
            cot[p, i] = (w_v[...] * og_v[:, at].astype(F32) * q_v[:, at].astype(F32)).astype(BF16)

    def hold_gv(p):
        @pl.loop(0, ny)
        def _(i):
            gv_own[p - down, i] = gv_v[:, cols(p, i)]

    def halves(src, dst, to):
        return [(src.at[pl.ds(a * pairs, pairs)], dst.at[pl.ds(a * pairs, pairs)], to) for a in range(2)]

    to_before, to_next = (ctx + nctx - 1) % nctx, (ctx + 1) % nctx

    def halo_halves(p):
        return halves(cot.at[p], halo.at[p], to_before)

    def gv_halves(p):
        return halves(gv_own.at[p - down], gv_in.at[p - down], to_next)

    own, after = pl.ds(0, 2 * rows), pl.ds(2 * rows, 2 * rows)
    back, back_high = pl.ds(4 * rows, 2 * rows), pl.ds(4 * rows, rows)

    def product(wave, other):
        a, b = wave[:rows], wave[rows:]
        e, f = other[:rows], other[rows:]
        return jnp.concatenate([a * e + b * f, b * e - a * f], axis=0)

    def inverse(both):
        top = both.astype(BF16)
        rest = (both - top.astype(F32)).astype(BF16)
        full = mul(tab[back, :], top)
        return full[:rows] + full[rows:] + mul(tab[back_high, :], rest)

    def spectra(p):
        @pl.loop(0, pairs, unroll=True)
        def _(k):
            cspec[p, k] = mul(tab[own, :], twice(jnp.concatenate([cot[p, 2 * k], cot[p, 2 * k + 1]], axis=1)))
            gv = jnp.concatenate([gv_v[:, cols(p, 2 * k)], gv_v[:, cols(p, 2 * k + 1)]], axis=1)
            gspec[p, k] = mul(tab[own, :], twice(gv))

    has_next = jnp.where(ctx == nctx - 1, 0.0, 1.0).astype(F32)
    has_before = jnp.where(ctx == 0, 0.0, 1.0).astype(F32)

    def with_halo(p, k):
        far = mul(tab[after, :], twice(jnp.concatenate([halo[p, 2 * k], halo[p, 2 * k + 1]], axis=1)))
        return cspec[p, k] + has_next * far

    def tap_sums(p):
        @pl.loop(0, pairs, unroll=True)
        def _(k):
            if p < down:
                wave = with_halo(p, k)
                cspec[p, k] = wave
                taps = inverse(product(wave, gspec[p, k]))
            else:
                u = p - down
                far = has_before * mul(tab[after, :], twice(jnp.concatenate([cot[p, 2 * k], cot[p, 2 * k + 1]], axis=1)))
                gv = mul(tab[own, :], twice(jnp.concatenate([gv_in[u, 2 * k], gv_in[u, 2 * k + 1]], axis=1)))
                taps = inverse(product(cspec[p, k], gspec[p, k]) + product(far, gv))
            for h in range(2):
                turned = taps[:, 128 * h:128 * (h + 1)].T
                for zz in range(2):
                    for ci in range(2):
                        at = zz * 64 + ci * 32
                        gst[p, ci, 2 * k + h, zz] = turned[at:at + 32]

    def values(p):
        @pl.loop(0, pairs, unroll=True)
        def _(k):
            f = jnp.concatenate(
                [fbuf[2 * k + h, 2 * p + zz] for h in range(2) for zz in range(2)], axis=0
            )
            fwave = lax.dot_general(
                tab[own, :], jnp.concatenate([f, f], axis=1), (((1,), (1,)), ((), ())),
                preferred_element_type=F32,
            )
            wave = cspec[p, k] if p < down else with_halo(p, k)
            out = inverse(product(wave, fwave)).astype(BF16)
            for h in range(2):
                v_v[:, cols(p, 2 * k + h)] = out[:, 128 * h:128 * (h + 1)]

        stores = []
        for i in range(ny):
            at = cols(p, i)
            stores.append(pltpu.make_async_copy(v_v.at[:, at], v_hbm.at[:, at], osem.at[p, i]))
            stores[-1].start()
        return stores

    def pair_stage(p):
        return [send(gst.at[p, 1 - c], r0.at[p], dp=2 * x + 1 - c)]

    def y_stage(p):
        @pl.loop(0, ny)
        def _(i):
            s0[p, i] = (gst[p, c, i] + r0[p, i]).astype(BF16)

        return [
            send(s0.at[p, (y + d) % ny], r2.at[p, d - 1], ctx=((y + d) % ny) * nz + z)
            for d in range(1, ny)
        ]

    def y_total(p):
        total = gst[p, c, y] + r0[p, y]
        for d in range(1, ny):
            total = total + r2[p, d - 1].astype(F32)
        s2[p] = total

    loads[5].wait()
    weight = jnp.where(tok[...] < 4, 1.0, 0.1).astype(F32)
    w_v[...] = jnp.broadcast_to(weight, (rows, rows)).T
    loads[0].wait()
    loads[1].wait()
    make_cot(0)
    loads[4].wait()
    hold_gv(down)
    loads[2].wait()
    pl.semaphore_wait(barrier, len(peers))

    fz = [send(fin.at[z], fin.at[z], ctx=y * nz + (z + d) % nz) for d in range(1, nz)]
    down_list = [(p, h) for p in range(chunks) for h in halo_halves(p)]
    up_list = [(p, h) for p in range(down, chunks) for h in gv_halves(p)]
    halos, gvs = {p: [] for p in range(chunks)}, {p: [] for p in range(chunks)}

    ways = ((down_list, halos, []), (up_list, gvs, []))
    sent = []

    def issue():
        for todo, done, flight in ways:
            if todo:
                p, (src, dst, to) = todo.pop(0)
                flight.append(send(src, dst, ctx=to))
                done[p].append(flight[-1])

    def pace():
        for todo, done, flight in ways:
            if todo:
                oldest = flight.pop(0)
                oldest.wait_send()
                sent.append(oldest)
        issue()

    issue()
    loads[3].wait()
    spectra(0)
    issue()
    for p in range(1, chunks):
        make_cot(p)
        if p > down:
            hold_gv(p)
    for p in range(1, chunks):
        spectra(p)
    pace()
    arrive(fz)
    fy = [
        send(fin.at[fhalf], fbuf.at[y, fhalf, frows], ctx=((y + d) % ny) * nz + z)
        for d in range(1, ny)
    ]
    fbuf[y, fhalf, frows] = fin[fhalf]
    pace()

    first, ys, stores = {}, {}, []
    for n, p in enumerate(order):
        arrive(halos[p] if p < down else gvs[p])
        tap_sums(p)
        first[p] = pair_stage(p)
        if n % 2:
            for r in order[n - 1:n + 1]:
                arrive(first[r])
                ys[r] = y_stage(r)
            pace()
            if n == 1:
                arrive(fy)
                fx = [
                    send(fbuf.at[:, fhalf, frows], fbuf.at[:, fhalf, frows], dp=2 * ((x + d) % nx) + c)
                    for d in range(1, nx)
                ]
            pace()
    arrive(fx)
    fc = [send(fbuf.at[:, fhalf], fbuf.at[:, fhalf], dp=2 * x + 1 - c)]
    for p in order[:-1]:
        arrive(ys[p])
        y_total(p)
    arrive(fc)
    stores += values(0)
    arrive(ys[order[-1]])
    y_total(order[-1])
    zs = []
    for d in range(1, nz):
        zi = (z + d) % nz
        zs.append(send(s2.at[zi // 2, zi % 2], r3.at[d - 1], ctx=y * nz + zi))
    for p in range(1, down):
        stores += values(p)
    for p in range(down, chunks - 1):
        arrive(halos[p])
        stores += values(p)
    arrive(zs)
    total = s2[z // 2, z % 2]
    for d in range(1, nz):
        total = total + r3[d - 1]
    fg[dp] = total * scale
    ds = [send(fg.at[dp], fg.at[dp], dp=(dp + d) % ndp) for d in range(1, ndp)]
    if chunks > 1:
        arrive(halos[chunks - 1])
        stores += values(chunks - 1)
    arrive(ds)
    for ci in range(2):
        total = fg[ci]
        for xi in range(1, nx):
            total = total + fg[2 * xi + ci]
        g_v[ci] = total
    result = pltpu.make_async_copy(g_v, g_hbm, lsem.at[6])
    result.start()
    for copy in started:
        if not any(copy is other for other in sent):
            copy.wait_send()
    for store in stores:
        store.wait()
    result.wait()


def body(token_ids, queries, gated_values, out_grad, filters):
    ndp, nctx = lax.axis_size("dp"), lax.axis_size("ctx")
    ny, nz = SIDES[nctx]
    nx = ndp // 2
    _, rows, wide = queries.shape
    assert wide == 64 * nctx and rows == 128
    chunks, pairs = nz // 2, ny // 2
    scale = float(ndp * nctx * rows) ** (-0.5)
    any_space = pl.BlockSpec(memory_space=pl.ANY)
    up = chunks // 2
    remote = chunks * (2 + ny) + 2 * up + 2 * (nz - 1) + (ny - 1) + nx + (ndp - 1)
    value_grad, filter_grad = pl.pallas_call(
        functools.partial(kernel, nx, ny, nz, scale),
        out_shape=(
            jax.ShapeDtypeStruct((rows, wide), BF16),
            jax.ShapeDtypeStruct((2, 32, rows), F32),
        ),
        in_specs=[any_space] * 6,
        out_specs=(any_space, any_space),
        scratch_shapes=[
            pltpu.VMEM((1, rows), jnp.int32),
            pltpu.VMEM((rows, wide), BF16),
            pltpu.VMEM((rows, wide), BF16),
            pltpu.VMEM((rows, wide), BF16),
            pltpu.VMEM((6 * rows, 2 * rows), BF16),
            pltpu.VMEM((rows, rows), F32),
            pltpu.VMEM((chunks, ny, rows, 128), BF16),
            pltpu.VMEM((chunks, ny, rows, 128), BF16),
            pltpu.VMEM((max(up, 1), ny, rows, 128), BF16),
            pltpu.VMEM((max(up, 1), ny, rows, 128), BF16),
            pltpu.VMEM((chunks, pairs, 2 * rows, 256), F32),
            pltpu.VMEM((chunks, pairs, 2 * rows, 256), F32),
            pltpu.VMEM((nz, 64 // nx, rows), BF16),
            pltpu.VMEM((ny, nz, 64, rows), BF16),
            pltpu.VMEM((rows, wide), BF16),
            pltpu.VMEM((chunks, 2, ny, 2, 32, rows), F32),
            pltpu.VMEM((chunks, ny, 2, 32, rows), F32),
            pltpu.VMEM((chunks, ny, 2, 32, rows), BF16),
            pltpu.VMEM((chunks, ny - 1, 2, 32, rows), BF16),
            pltpu.VMEM((chunks, 2, 32, rows), F32),
            pltpu.VMEM((nz - 1, 32, rows), F32),
            pltpu.VMEM((ndp, 32, rows), F32),
            pltpu.VMEM((2, 32, rows), F32),
            pltpu.SemaphoreType.DMA((7,)),
            pltpu.SemaphoreType.DMA((chunks, ny)),
            pltpu.SemaphoreType.DMA((remote,)),
            pltpu.SemaphoreType.DMA((remote,)),
        ],
        compiler_params=pltpu.CompilerParams(
            collective_id=0, has_side_effects=True, vmem_limit_bytes=60 * 1024 * 1024
        ),
        name="mixer_backward",
    )(
        token_ids, queries[0], gated_values[0], out_grad[0], filters, jnp.asarray(tables(rows)),
    )
    return value_grad[None], filter_grad.reshape(64, rows)


def solution(mesh):
    return jax.shard_map(
        body,
        mesh=mesh,
        in_specs=(
            P("dp", "ctx"),
            P("dp", "ctx", None),
            P("dp", "ctx", None),
            P("dp", "ctx", None),
            P("ctx", None),
        ),
        out_specs=(P("dp", "ctx", None), P("ctx", None)),
        check_vma=False,
    )
```

```python
import functools

import jax
import jax.numpy as jnp
import numpy as np
from jax import lax
from jax.experimental import pallas as pl
from jax.experimental.pallas import tpu as pltpu
from jax.sharding import PartitionSpec as P

F32, BF16 = jnp.float32, jnp.bfloat16
SIDES = {64: (8, 8)}


def tables(rows):
    span = 2 * rows
    angle = np.pi * (2 * np.arange(rows)[:, None] + 1) * np.arange(span)[None, :] / span
    wave = np.concatenate([np.cos(angle), np.sin(angle)], axis=0)
    high = wave.astype(BF16)
    low = (wave - high.astype(np.float64)).astype(BF16)
    own = np.concatenate([high[:, :rows], low[:, :rows]], axis=1)
    after = np.concatenate([high[:, rows:], low[:, rows:]], axis=1)
    back = np.concatenate([high[:, :rows].T, low[:, :rows].T], axis=0)
    back = (back.astype(np.float64) / rows).astype(BF16)
    return np.concatenate([own, after, back], axis=0)


def mul(a, b):
    return jnp.dot(a, b, preferred_element_type=F32)


def twice(x):
    return jnp.concatenate([x, x], axis=0)


def kernel(
    nx, ny, nz, scale,
    tok_hbm, q_hbm, gv_hbm, og_hbm, filt_hbm, tab_hbm,
    v_hbm, g_hbm,
    tok, q_v, og_v, gv_v, tab, w_v, cot, halo, gv_own, gv_in, cspec, gspec, fin, fbuf, v_v,
    gst, r0, s0, r2, s2, sz, r3, fg, g_v,
    lsem, osem, ssem, rsem,
):
    rows = q_v.shape[0]
    chunks = nz // 2
    pairs = ny // 2
    dp, ctx = lax.axis_index("dp"), lax.axis_index("ctx")
    x, c = dp // 2, dp % 2
    y, z = ctx // nz, ctx % nz
    nctx, ndp = ny * nz, 2 * nx
    frows = pl.ds(pl.multiple_of(x * (64 // nx), 16), 64 // nx)
    fhalf = pl.ds(c * (nz // 2), nz // 2)
    down = chunks - chunks // 2
    order = [p for k in range(down) for p in (k, down + k) if p < chunks]

    barrier = pltpu.get_barrier_semaphore()
    peers = [{"ctx": (ctx + 1) % nctx}, {"ctx": (ctx + nctx - 1) % nctx}]
    peers += [{"dp": (dp + d) % ndp} for d in range(1, ndp)]
    peers += [{"ctx": ((y + d) % ny) * nz + z} for d in range(1, ny)]
    peers += [{"ctx": y * nz + (z + d) % nz} for d in range(1, nz)]
    for peer in peers:
        pl.semaphore_signal(barrier, inc=1, device_id=peer, device_id_type=pl.DeviceIdType.MESH)

    loads = [
        pltpu.make_async_copy(q_hbm, q_v, lsem.at[0]),
        pltpu.make_async_copy(og_hbm, og_v, lsem.at[1]),
        pltpu.make_async_copy(filt_hbm.at[frows], fin.at[z], lsem.at[2]),
        pltpu.make_async_copy(tab_hbm, tab, lsem.at[3]),
        pltpu.make_async_copy(gv_hbm, gv_v, lsem.at[4]),
        pltpu.make_async_copy(tok_hbm, tok, lsem.at[5]),
    ]
    for load in loads:
        load.start()

    started = []

    def send(src, dst, **where):
        n = len(started)
        copy = pltpu.make_async_remote_copy(
            src_ref=src, dst_ref=dst, send_sem=ssem.at[n], recv_sem=rsem.at[n],
            device_id=where, device_id_type=pl.DeviceIdType.MESH,
        )
        copy.start()
        started.append(copy)
        return copy

    def arrive(copies):
        for copy in copies:
            copy.wait_recv()

    def cols(p, i):
        return pl.ds(pl.multiple_of(i * (nz * 64) + p * 128, 128), 128)

    def make_cot(p):
        @pl.loop(0, ny)
        def _(i):
            at = cols(p, i)
            cot[p, i] = (w_v[...] * og_v[:, at].astype(F32) * q_v[:, at].astype(F32)).astype(BF16)

    def hold_gv(p):
        @pl.loop(0, ny)
        def _(i):
            gv_own[p - down, i] = gv_v[:, cols(p, i)]

    def halves(src, dst, to):
        return [(src.at[pl.ds(a * pairs, pairs)], dst.at[pl.ds(a * pairs, pairs)], to) for a in range(2)]

    to_before, to_next = (ctx + nctx - 1) % nctx, (ctx + 1) % nctx

    def halo_halves(p):
        return halves(cot.at[p], halo.at[p], to_before)

    def gv_halves(p):
        return halves(gv_own.at[p - down], gv_in.at[p - down], to_next)

    own, after = pl.ds(0, 2 * rows), pl.ds(2 * rows, 2 * rows)
    back, back_high = pl.ds(4 * rows, 2 * rows), pl.ds(4 * rows, rows)

    def product(wave, other):
        a, b = wave[:rows], wave[rows:]
        e, f = other[:rows], other[rows:]
        return jnp.concatenate([a * e + b * f, b * e - a * f], axis=0)

    def inverse(both):
        top = both.astype(BF16)
        rest = (both - top.astype(F32)).astype(BF16)
        full = mul(tab[back, :], top)
        return full[:rows] + full[rows:] + mul(tab[back_high, :], rest)

    def spectra(p):
        @pl.loop(0, pairs, unroll=True)
        def _(k):
            cspec[p, k] = mul(tab[own, :], twice(jnp.concatenate([cot[p, 2 * k], cot[p, 2 * k + 1]], axis=1)))
            gv = jnp.concatenate([gv_v[:, cols(p, 2 * k)], gv_v[:, cols(p, 2 * k + 1)]], axis=1)
            gspec[p, k] = mul(tab[own, :], twice(gv))

    has_next = jnp.where(ctx == nctx - 1, 0.0, 1.0).astype(F32)
    has_before = jnp.where(ctx == 0, 0.0, 1.0).astype(F32)

    def with_halo(p, k):
        far = mul(tab[after, :], twice(jnp.concatenate([halo[p, 2 * k], halo[p, 2 * k + 1]], axis=1)))
        return cspec[p, k] + has_next * far

    def tap_sums(p):
        @pl.loop(0, pairs, unroll=True)
        def _(k):
            if p < down:
                wave = with_halo(p, k)
                cspec[p, k] = wave
                taps = inverse(product(wave, gspec[p, k]))
            else:
                u = p - down
                far = has_before * mul(tab[after, :], twice(jnp.concatenate([cot[p, 2 * k], cot[p, 2 * k + 1]], axis=1)))
                gv = mul(tab[own, :], twice(jnp.concatenate([gv_in[u, 2 * k], gv_in[u, 2 * k + 1]], axis=1)))
                taps = inverse(product(cspec[p, k], gspec[p, k]) + product(far, gv))
            for h in range(2):
                turned = taps[:, 128 * h:128 * (h + 1)].T
                for zz in range(2):
                    for ci in range(2):
                        at = zz * 64 + ci * 32
                        gst[p, ci, 2 * k + h, zz] = turned[at:at + 32]

    def values(p):
        @pl.loop(0, pairs, unroll=True)
        def _(k):
            f = jnp.concatenate(
                [fbuf[2 * k + h, 2 * p + zz] for h in range(2) for zz in range(2)], axis=0
            )
            fwave = lax.dot_general(
                tab[own, :], jnp.concatenate([f, f], axis=1), (((1,), (1,)), ((), ())),
                preferred_element_type=F32,
            )
            wave = cspec[p, k] if p < down else with_halo(p, k)
            out = inverse(product(wave, fwave)).astype(BF16)
            for h in range(2):
                v_v[:, cols(p, 2 * k + h)] = out[:, 128 * h:128 * (h + 1)]

        stores = []
        for i in range(ny):
            at = cols(p, i)
            stores.append(pltpu.make_async_copy(v_v.at[:, at], v_hbm.at[:, at], osem.at[p, i]))
            stores[-1].start()
        return stores

    def pair_stage(p):
        return [send(gst.at[p, 1 - c], r0.at[p], dp=2 * x + 1 - c)]

    def y_stage(p):
        @pl.loop(0, ny)
        def _(i):
            s0[p, i] = (gst[p, c, i] + r0[p, i]).astype(BF16)

        return [
            send(s0.at[p, (y + d) % ny], r2.at[p, d - 1], ctx=((y + d) % ny) * nz + z)
            for d in range(1, ny)
        ]

    def y_total(p):
        total = gst[p, c, y] + r0[p, y]
        for d in range(1, ny):
            total = total + r2[p, d - 1].astype(F32)
        s2[p] = total
        sz[p] = total.astype(BF16)

    loads[5].wait()
    weight = jnp.where(tok[...] < 4, 1.0, 0.1).astype(F32)
    w_v[...] = jnp.broadcast_to(weight, (rows, rows)).T
    loads[0].wait()
    loads[1].wait()
    make_cot(0)
    loads[4].wait()
    hold_gv(down)
    loads[2].wait()
    pl.semaphore_wait(barrier, len(peers))

    fz = [send(fin.at[z], fin.at[z], ctx=y * nz + (z + d) % nz) for d in range(1, nz)]
    down_list = [(p, h) for p in range(chunks) for h in halo_halves(p)]
    up_list = [(p, h) for p in range(down, chunks) for h in gv_halves(p)]
    halos, gvs = {p: [] for p in range(chunks)}, {p: [] for p in range(chunks)}

    ways = ((down_list, halos, []), (up_list, gvs, []))
    sent = []

    def issue():
        for todo, done, flight in ways:
            if todo:
                p, (src, dst, to) = todo.pop(0)
                flight.append(send(src, dst, ctx=to))
                done[p].append(flight[-1])

    def pace():
        for todo, done, flight in ways:
            if todo:
                oldest = flight.pop(0)
                oldest.wait_send()
                sent.append(oldest)
        issue()

    issue()
    loads[3].wait()
    spectra(0)
    issue()
    for p in range(1, chunks):
        make_cot(p)
        if p > down:
            hold_gv(p)
    for p in range(1, chunks):
        spectra(p)
    pace()
    arrive(fz)
    fy = [
        send(fin.at[fhalf], fbuf.at[y, fhalf, frows], ctx=((y + d) % ny) * nz + z)
        for d in range(1, ny)
    ]
    fbuf[y, fhalf, frows] = fin[fhalf]
    pace()

    first, ys, stores = {}, {}, []
    for n, p in enumerate(order):
        arrive(halos[p] if p < down else gvs[p])
        tap_sums(p)
        first[p] = pair_stage(p)
        if n % 2:
            for r in order[n - 1:n + 1]:
                arrive(first[r])
                ys[r] = y_stage(r)
            pace()
            pace()
    arrive(fy)
    fx = [
        send(fbuf.at[:, fhalf, frows], fbuf.at[:, fhalf, frows], dp=2 * ((x + d) % nx) + c)
        for d in range(1, nx)
    ]
    for p in order:
        arrive(ys[p])
        y_total(p)
    zs = []
    for d in range(1, nz):
        zi = (z + d) % nz
        zs.append(send(sz.at[zi // 2, zi % 2], r3.at[d - 1], ctx=y * nz + zi))
    arrive(fx)
    fc = [send(fbuf.at[:, fhalf], fbuf.at[:, fhalf], dp=2 * x + 1 - c)]
    arrive(fc)
    for p in range(down):
        stores += values(p)
    for p in range(down, chunks - 1):
        arrive(halos[p])
        stores += values(p)
    arrive(zs)
    total = s2[z // 2, z % 2]
    for d in range(1, nz):
        total = total + r3[d - 1].astype(F32)
    fg[dp] = total * scale
    ds = [send(fg.at[dp], fg.at[dp], dp=(dp + d) % ndp) for d in range(1, ndp)]
    if chunks > 1:
        arrive(halos[chunks - 1])
        stores += values(chunks - 1)
    arrive(ds)
    for ci in range(2):
        total = fg[ci]
        for xi in range(1, nx):
            total = total + fg[2 * xi + ci]
        g_v[ci] = total
    result = pltpu.make_async_copy(g_v, g_hbm, lsem.at[6])
    result.start()
    for copy in started:
        if not any(copy is other for other in sent):
            copy.wait_send()
    for store in stores:
        store.wait()
    result.wait()


def body(token_ids, queries, gated_values, out_grad, filters):
    ndp, nctx = lax.axis_size("dp"), lax.axis_size("ctx")
    ny, nz = SIDES[nctx]
    nx = ndp // 2
    _, rows, wide = queries.shape
    assert wide == 64 * nctx and rows == 128
    chunks, pairs = nz // 2, ny // 2
    scale = float(ndp * nctx * rows) ** (-0.5)
    any_space = pl.BlockSpec(memory_space=pl.ANY)
    up = chunks // 2
    remote = chunks * (2 + ny) + 2 * up + 2 * (nz - 1) + (ny - 1) + nx + (ndp - 1)
    value_grad, filter_grad = pl.pallas_call(
        functools.partial(kernel, nx, ny, nz, scale),
        out_shape=(
            jax.ShapeDtypeStruct((rows, wide), BF16),
            jax.ShapeDtypeStruct((2, 32, rows), F32),
        ),
        in_specs=[any_space] * 6,
        out_specs=(any_space, any_space),
        scratch_shapes=[
            pltpu.VMEM((1, rows), jnp.int32),
            pltpu.VMEM((rows, wide), BF16),
            pltpu.VMEM((rows, wide), BF16),
            pltpu.VMEM((rows, wide), BF16),
            pltpu.VMEM((6 * rows, 2 * rows), BF16),
            pltpu.VMEM((rows, rows), F32),
            pltpu.VMEM((chunks, ny, rows, 128), BF16),
            pltpu.VMEM((chunks, ny, rows, 128), BF16),
            pltpu.VMEM((max(up, 1), ny, rows, 128), BF16),
            pltpu.VMEM((max(up, 1), ny, rows, 128), BF16),
            pltpu.VMEM((chunks, pairs, 2 * rows, 256), F32),
            pltpu.VMEM((chunks, pairs, 2 * rows, 256), F32),
            pltpu.VMEM((nz, 64 // nx, rows), BF16),
            pltpu.VMEM((ny, nz, 64, rows), BF16),
            pltpu.VMEM((rows, wide), BF16),
            pltpu.VMEM((chunks, 2, ny, 2, 32, rows), F32),
            pltpu.VMEM((chunks, ny, 2, 32, rows), F32),
            pltpu.VMEM((chunks, ny, 2, 32, rows), BF16),
            pltpu.VMEM((chunks, ny - 1, 2, 32, rows), BF16),
            pltpu.VMEM((chunks, 2, 32, rows), F32),
            pltpu.VMEM((chunks, 2, 32, rows), BF16),
            pltpu.VMEM((nz - 1, 32, rows), BF16),
            pltpu.VMEM((ndp, 32, rows), F32),
            pltpu.VMEM((2, 32, rows), F32),
            pltpu.SemaphoreType.DMA((7,)),
            pltpu.SemaphoreType.DMA((chunks, ny)),
            pltpu.SemaphoreType.DMA((remote,)),
            pltpu.SemaphoreType.DMA((remote,)),
        ],
        compiler_params=pltpu.CompilerParams(
            collective_id=0, has_side_effects=True, vmem_limit_bytes=60 * 1024 * 1024
        ),
        name="mixer_backward",
    )(
        token_ids, queries[0], gated_values[0], out_grad[0], filters, jnp.asarray(tables(rows)),
    )
    return value_grad[None], filter_grad.reshape(64, rows)


def solution(mesh):
    return jax.shard_map(
        body,
        mesh=mesh,
        in_specs=(
            P("dp", "ctx"),
            P("dp", "ctx", None),
            P("dp", "ctx", None),
            P("dp", "ctx", None),
            P("ctx", None),
        ),
        out_specs=(P("dp", "ctx", None), P("ctx", None)),
        check_vma=False,
    )
```
